32 devices in a mesh: orient: 8 (over y, x, core), strip: 4 (over z).
Axes of the slice: x: 2, y: 2, z: 4, core: 2. Of those that a mesh axis runs over, the one named last changes fastest.
Arguments:
- inflow_field: bfloat16 [32, 8, 32, 512], P('orient', None, 'strip'), may hold values from -6 to 6
- kernel_one: bfloat16 [32, 9, 8, 8], replicated, may hold values from -0.125 to 0.125
- kernel_two: bfloat16 [32, 9, 8, 8], replicated, may hold values from -0.125 to 0.125
- turbine_mask: int32 [32, 512], P('strip'), may hold values 0 or 1
- wind_sector: int32 [1], replicated, may hold values from 0 to 31
- wake_cotangent: bfloat16 [32, 8, 32, 512], P('orient', None, 'strip'), may hold values from -6 to 6
Outputs:
- wake_out: bfloat16 [32, 8, 32, 512], P('orient', None, 'strip')
- kernel_grad_one: float32 [32, 9, 8, 8], replicated
- kernel_grad_two: float32 [32, 9, 8, 8], replicated
The draws below stay inside these ranges and needn't reach their ends.
Inputs may be any that keep to these rules, and one draw needn't show every extreme that they name: `wind_sector`: names one element of the group.
All inputs are finite; a program needn't handle non-finite values. No bound on the sum of `turbine_mask` on one device may be relied on, other than what follows from the above.
Results may differ from the reference program's by a relative error of at most 0.0051.
Values may be sent and summed in bfloat16 or wider, within the bound.
A program may use at most 128 MiB of HBM per device.

```python
import math
import jax
import jax.numpy as jnp
from jax import lax

G = 32
CH = 8
TAPS = 9
COLS = 512
ROWS = 32


def touch_ends(array, rng, low, high):
    place = [jax.random.randint(jax.random.fold_in(rng, axis), (), 0, length) for axis, length in enumerate(array.shape)]
    main_axis = array.shape.index(max(array.shape))
    beside = place[:main_axis] + [(place[main_axis] + 1) % array.shape[main_axis]] + place[main_axis + 1:]
    return array.at[tuple(place)].set(low).at[tuple(beside)].set(high)


def level_of(own_key, dims, cuts, least, largest):
    level, own = 1.0, jax.random.fold_in(own_key, 6)
    for position, blocks in cuts:
        draws = jnp.exp(jax.random.uniform(jax.random.fold_in(own, position), (blocks,), jnp.float32, least / len(cuts), largest / len(cuts)))
        level = level * jnp.repeat(draws, dims[position] // blocks).reshape([-1 if axis == position else 1 for axis in range(len(dims))])
    return level


def normal_values(own_key, dims, scale, most, cuts=(), held_as=jnp.bfloat16):
    result = jax.random.normal(own_key, dims, jnp.float32) * scale
    if len(cuts) > 0:
        result = level_of(own_key, dims, cuts, -0.22, 0.18) * result
    return jnp.clip(result, min=-most, max=most).astype(held_as)


def setup_inputs(seed: int = 0) -> dict:
    key_of = jax.random.split(jax.random.key(seed), 7)
    return {
        "inflow_field": normal_values(key_of[0], (G, CH, ROWS, COLS), 1.0, 6.0, ((0, 8), (2, 4))),
        "kernel_one": normal_values(key_of[1], (G, TAPS, CH, CH), (G * TAPS * CH) ** -0.5, 0.125),
        "kernel_two": normal_values(key_of[2], (G, TAPS, CH, CH), (G * TAPS * CH) ** -0.5, 0.125),
        "turbine_mask": touch_ends((jax.random.randint(key_of[3], (ROWS, COLS), 0, 8) < 1).astype(jnp.int32), jax.random.fold_in(key_of[3], 1), 0, 1),
        "wind_sector": jax.random.randint(key_of[4], (1,), 0, G).astype(jnp.int32),
        "wake_cotangent": normal_values(key_of[5], (G, CH, ROWS, COLS), 1.0, 6.0, ((0, 8), (2, 4))),
    }


OFFSETS = ((0, 0), (0, 1), (0, 2), (1, 0), (1, 1), (1, 2), (2, 0), (2, 1), (2, 2))

def relative(row_ids, col_ids, sector):
    halfway = G // 2
    row_rot = row_ids % halfway
    row_ref = row_ids // halfway
    col_rot = col_ids % halfway
    col_ref = col_ids // halfway
    sec_rot = sector % halfway
    sec_ref = sector // halfway
    moved_rot = (sec_rot + (1 - 2 * sec_ref) * col_rot) % halfway
    moved_ref = (sec_ref + col_ref) % 2
    inverse_rot = jnp.where(row_ref == 0, (halfway - row_rot) % halfway, row_rot)
    result_rot = (inverse_rot + (1 - 2 * row_ref) * moved_rot) % halfway
    result_ref = (row_ref + moved_ref) % 2
    return (result_ref * halfway + result_rot).astype(jnp.int32)

def kernel_block(kernel, row_ids, col_ids, sector):
    channels = kernel.shape[2]
    tap_count = kernel.shape[1]
    relation = relative(row_ids[:, None], col_ids[None, :], sector).reshape(-1)
    onehot = (relation[:, None] == jnp.arange(G, dtype=jnp.int32)[None, :]).astype(jnp.bfloat16)
    picked = jnp.dot(onehot, kernel.reshape(G, -1), preferred_element_type=jnp.float32)
    picked = picked.reshape(row_ids.shape[0], col_ids.shape[0], tap_count, channels, channels)
    picked = picked.transpose(2, 0, 3, 1, 4)
    return picked.reshape(tap_count, row_ids.shape[0] * channels, col_ids.shape[0] * channels).astype(jnp.bfloat16)

def fold_kernel(partial_grad, row_ids, col_ids, sector):
    tap_count = partial_grad.shape[0]
    channels = partial_grad.shape[1] // row_ids.shape[0]
    relation = relative(row_ids[:, None], col_ids[None, :], sector).reshape(-1)
    onehot = (relation[:, None] == jnp.arange(G, dtype=jnp.int32)[None, :]).astype(jnp.float32)
    arranged = partial_grad.reshape(tap_count, row_ids.shape[0], channels, col_ids.shape[0], channels)
    arranged = arranged.transpose(1, 3, 0, 2, 4).reshape(relation.shape[0], -1)
    folded = jnp.dot(onehot.T, arranged, precision=lax.Precision.HIGHEST, preferred_element_type=jnp.float32)
    return folded.reshape(G, tap_count, channels, channels)

def conv_forward(source, weights):
    full_width, height, extent = source.shape
    padded = jnp.pad(source, ((0, 0), (1, 1), (1, 1)))
    summed = jnp.zeros((weights.shape[1], height * extent), jnp.float32)
    for tap_index, (row_shift, col_shift) in enumerate(OFFSETS):
        window = padded[:, row_shift:row_shift + height, col_shift:col_shift + extent].reshape(full_width, -1)
        summed = summed + jnp.dot(weights[tap_index], window, preferred_element_type=jnp.float32)
    return summed.reshape(-1, height, extent)

def conv_backward(gradient, weights):
    full_width, height, extent = gradient.shape
    padded = jnp.pad(gradient, ((0, 0), (1, 1), (1, 1)))
    summed = jnp.zeros((weights.shape[2], height * extent), jnp.float32)
    for tap_index, (row_shift, col_shift) in enumerate(OFFSETS):
        window = padded[:, 2 - row_shift:2 - row_shift + height, 2 - col_shift:2 - col_shift + extent].reshape(full_width, -1)
        summed = summed + jnp.dot(weights[tap_index].T, window, preferred_element_type=jnp.float32)
    return summed.reshape(-1, height, extent)

def weight_grad(gradient, source):
    full_width, height, extent = source.shape
    padded = jnp.pad(source, ((0, 0), (1, 1), (1, 1)))
    flat_grad = gradient.reshape(gradient.shape[0], -1)
    pieces = []
    for row_shift, col_shift in OFFSETS:
        window = padded[:, row_shift:row_shift + height, col_shift:col_shift + extent].reshape(full_width, -1)
        pieces.append(lax.dot_general(flat_grad, window, (((1,), (1,)), ((), ())), preferred_element_type=jnp.float32))
    return jnp.stack(pieces, 0)

def reference(inflow_field, kernel_one, kernel_two, turbine_mask, wind_sector, wake_cotangent):
    full_width = G * CH
    sector = wind_sector[0]
    neutral = jnp.int32(0)
    groups = jnp.arange(G, dtype=jnp.int32)
    weights_one = kernel_block(kernel_one, groups, groups, sector)
    weights_two = kernel_block(kernel_two, groups, groups, neutral)
    open_cells = (1 - turbine_mask).astype(jnp.float32)
    source = inflow_field.reshape(full_width, ROWS, COLS)
    first_pre = conv_forward(source, weights_one)
    sigmoid_one = jax.nn.sigmoid(first_pre)
    hidden = (first_pre * sigmoid_one * open_cells).astype(jnp.bfloat16)
    second_pre = conv_forward(hidden, weights_two)
    wake_out = second_pre.astype(jnp.bfloat16).reshape(G, CH, ROWS, COLS)
    cotangent = wake_cotangent.reshape(full_width, ROWS, COLS)
    scale_factor = 1.0 / math.sqrt(G * ROWS * COLS)
    grad_two = fold_kernel(weight_grad(cotangent, hidden), groups, groups, neutral) * scale_factor
    back_grad = conv_backward(cotangent, weights_two)
    first_grad = (back_grad * open_cells * sigmoid_one * (1.0 + first_pre * (1.0 - sigmoid_one))).astype(jnp.bfloat16)
    grad_one = fold_kernel(weight_grad(first_grad, source), groups, groups, sector) * scale_factor
    return (wake_out, grad_one, grad_two)
```

```python
import functools
import math

import jax
import jax.numpy as jnp
from jax import lax
from jax.experimental import pallas as pl
from jax.experimental.pallas import tpu as pltpu
from jax.sharding import PartitionSpec as P

G = 32
HALF = 16
LANES = 128
BF16 = jnp.bfloat16
F32 = jnp.float32


def relative(row_ids, col_ids, sector):
    row_rot = row_ids % HALF
    row_ref = row_ids // HALF
    col_rot = col_ids % HALF
    col_ref = col_ids // HALF
    sec_rot = sector % HALF
    sec_ref = sector // HALF
    moved_rot = (sec_rot + (1 - 2 * sec_ref) * col_rot) % HALF
    moved_ref = (sec_ref + col_ref) % 2
    inverse_rot = jnp.where(row_ref == 0, (HALF - row_rot) % HALF, row_rot)
    result_rot = (inverse_rot + (1 - 2 * row_ref) * moved_rot) % HALF
    result_ref = (row_ref + moved_ref) % 2
    return result_ref * HALF + result_rot


def build_weights(bases, at, dst, flip):
    for s in range(2):
        for m in range(dst.shape[1] // LANES):
            cols = slice(m * LANES, (m + 1) * LANES)
            base = bases[at + s, :, cols]
            turned = [base if r == 0 else pltpu.roll(base, 8 * r, 1) for r in range(HALF)]
            if flip is not None:
                turned = [jnp.where(flip, turned[-r % HALF], turned[r]) for r in range(HALF)]
            for r in range(0, HALF, 2):
                both = jnp.concatenate([turned[r], turned[r + 1]], axis=0).astype(BF16)
                row = (s * HALF + r) * 8
                dst[row : row + 16, cols] = both


def fold(product, out, tap_row, flip):
    for b in range(3):
        for sg in range(2):
            lane = slice(sg * LANES, (sg + 1) * LANES)
            for sh in range(2):
                total = None
                for r in range(HALF):
                    row = b * 256 + (sh * HALF + r) * 8
                    piece = product[row : row + 8, lane]
                    if r > 0:
                        back = pltpu.roll(piece, LANES - 8 * r, 1)
                        if flip is not None:
                            back = jnp.where(flip, pltpu.roll(piece, 8 * r, 1), back)
                        piece = back
                    total = piece if total is None else total + piece
                at = (tap_row * 3 + b) * 256 + sg * LANES
                out[sh, :, at : at + LANES] = total


def shifted(value, by):
    if by == 0:
        return value
    return pltpu.roll(value.astype(F32), by % LANES, 1).astype(BF16)


def stack_shifts(src, dst, first, count, sign):
    for i in range(first, first + count):
        cols = slice(i * LANES, (i + 1) * LANES)
        value = src[:, cols]
        for b in range(3):
            dst[b * 256 : (b + 1) * 256, cols] = shifted(value, sign * (1 - b))


def dot(a, b):
    return jnp.dot(a, b, preferred_element_type=F32)


def dot_nt(a, b):
    return lax.dot_general(a, b, (((1,), (1,)), ((), ())), preferred_element_type=F32)


def compute(width, bases, turn, opened, x, cot, wake, t1, t2, w1, w2, w2t, xs, hs, cs, dfac, hid, own, prod):
    flip = turn[...] > 0.5
    build_weights(bases, 0, w1, flip)
    build_weights(bases, 2, w2, None)
    build_weights(bases, 4, w2t, None)
    lane = lax.broadcasted_iota(jnp.int32, (256, LANES), 1)
    inner = (lane >= 2) & (lane < 2 + width)
    stack_shifts(x, xs, 0, 12, 1)
    for n in range(5):
        total = sum(
            dot(w1[:, a * 768 : (a + 1) * 768], xs[:, (2 * n + a) * LANES : (2 * n + a + 2) * LANES])
            for a in range(3)
        )
        cols = slice(2 * n * LANES, (2 * n + 2) * LANES)
        free = opened[0:1, cols]
        sig = jax.nn.sigmoid(total)
        hid[:, cols] = (total * sig * free).astype(BF16)
        dfac[:, cols] = free * sig * (1.0 + total * (1.0 - sig))
    stack_shifts(hid, hs, 0, 10, 1)
    for n in range(4):
        total = sum(
            dot(w2[:, a * 768 : (a + 1) * 768], hs[:, (2 * n + a) * LANES : (2 * n + a + 2) * LANES])
            for a in range(3)
        )
        wake[:, 2 * n * LANES : (2 * n + 2) * LANES] = total.astype(BF16)
    stack_shifts(cot, cs, 0, 10, -1)
    for i in range(8):
        value = cot[:, (i + 1) * LANES : (i + 2) * LANES].astype(F32)
        own[:, i * LANES : (i + 1) * LANES] = jnp.where(inner, value, 0.0).astype(BF16)
    for a in range(3):
        prod[...] = dot_nt(hs[:, a * LANES : (a + 8) * LANES], own[...])
        fold(prod, t2, a, None)
    for n in range(4):
        total = sum(
            dot(
                w2t[:, a * 768 : (a + 1) * 768],
                cs[:, (2 * n + 2 - a) * LANES : (2 * n + 4 - a) * LANES],
            )
            for a in range(3)
        )
        cols = slice((2 * n + 1) * LANES, (2 * n + 3) * LANES)
        total = total * dfac[:, cols]
        for i in range(2):
            value = jnp.where(inner, total[:, i * LANES : (i + 1) * LANES], 0.0)
            own[:, (2 * n + i) * LANES : (2 * n + i + 1) * LANES] = value.astype(BF16)
    for a in range(3):
        prod[...] = dot_nt(xs[:, (a + 1) * LANES : (a + 9) * LANES], own[...])
        fold(prod, t1, a, flip)


def local_kernel(width, bases, turn, opened, x, cot):
    vmem = pl.BlockSpec(memory_space=pltpu.VMEM)
    return pl.pallas_call(
        functools.partial(compute, width),
        out_shape=(
            jax.ShapeDtypeStruct((256, 8 * LANES), BF16),
            jax.ShapeDtypeStruct((2, 8, 2304), F32),
            jax.ShapeDtypeStruct((2, 8, 2304), F32),
        ),
        in_specs=[vmem] * 5,
        out_specs=(vmem,) * 3,
        scratch_shapes=[
            pltpu.VMEM((256, 2304), BF16),
            pltpu.VMEM((256, 2304), BF16),
            pltpu.VMEM((256, 2304), BF16),
            pltpu.VMEM((768, 12 * LANES), BF16),
            pltpu.VMEM((768, 10 * LANES), BF16),
            pltpu.VMEM((768, 10 * LANES), BF16),
            pltpu.VMEM((256, 10 * LANES), F32),
            pltpu.VMEM((256, 10 * LANES), BF16),
            pltpu.VMEM((256, 8 * LANES), BF16),
            pltpu.VMEM((768, 256), F32),
        ],
        compiler_params=pltpu.CompilerParams(vmem_limit_bytes=48 * 1024 * 1024),
    )(bases, turn, opened, x, cot)


def windows(padded, width):
    step = (padded.shape[-1] - 4) // width
    rest = [(0, 0)] * (padded.ndim - 1) + [(0, LANES - step - 4)]
    pieces = [jnp.pad(padded[..., step * i : step * i + step + 4], rest) for i in range(width)]
    return jnp.stack(pieces, 0)


def edges(rows, width):
    count = lax.axis_size("strip")
    height = rows.shape[-2]
    up = [(i, i + 1) for i in range(count - 1)]
    down = [(i + 1, i) for i in range(count - 1)]
    before = lax.ppermute(rows[..., height - width :, :], "strip", up)
    after = lax.ppermute(rows[..., :width, :], "strip", down)
    return jnp.concatenate([before, rows, after], axis=-2)


def turned_bank(bank, sector, transposed):
    ids = jnp.arange(G, dtype=jnp.int32)
    pair = jnp.array([0, HALF], jnp.int32)
    if transposed:
        relation = relative(ids[None, :], pair[:, None], sector)
    else:
        relation = relative(pair[:, None], ids[None, :], sector)
    onehot = (relation.reshape(-1)[:, None] == ids[None, :]).astype(BF16)
    picked = jnp.dot(onehot, bank.reshape(G, -1), preferred_element_type=F32)
    picked = picked.reshape(2, G, 9, 8, 8)
    order = (0, 4, 2, 1, 3) if transposed else (0, 3, 2, 1, 4)
    return picked.transpose(order).reshape(2, 8, 2304)


def unfold(folded, sector):
    ids = jnp.arange(HALF, dtype=jnp.int32)
    sec_rot, sec_ref = sector % HALF, sector // HALF
    sh = jnp.arange(2, dtype=jnp.int32)[:, None, None]
    sg = jnp.arange(2, dtype=jnp.int32)[None, :, None]
    j = ids[None, None, :]
    turn = (sh + sec_ref) % 2
    rot = jnp.where(sg == 0, sec_rot - j + HALF, j - sec_rot + HALF) % HALF
    element = (((turn + sg) % 2) * HALF + rot).reshape(-1)
    onehot = (jnp.arange(G, dtype=jnp.int32)[:, None] == element[None, :]).astype(F32)
    parts = folded.reshape(2, 8, 9, 2, HALF, 8).transpose(0, 3, 4, 2, 5, 1).reshape(64, 576)
    full = jnp.dot(onehot, parts, precision=lax.Precision.HIGHEST, preferred_element_type=F32)
    return full.reshape(G, 9, 8, 8)


def shards(inflow_field, kernel_one, kernel_two, turbine_mask, wind_sector, wake_cotangent):
    groups, channels, height, extent = inflow_field.shape
    local = groups * channels
    devices = lax.axis_size("orient")
    sector = wind_sector[0]
    neutral = jnp.int32(0)
    scale = 1.0 / math.sqrt(G * height * lax.axis_size("strip") * extent)
    bases = jnp.concatenate(
        [
            turned_bank(kernel_one, sector, False),
            turned_bank(kernel_two, neutral, False),
            turned_bank(kernel_two, neutral, True),
        ],
        0,
    )
    turn = jnp.broadcast_to((sector // HALF).astype(F32), (8, LANES))
    both = jnp.stack([inflow_field, wake_cotangent], 0).reshape(2, local, height, extent)
    both = jnp.pad(both, ((0, 0), (0, 0), (0, 0), (2, 2)))
    packed = windows(both, devices)
    spread = lax.all_to_all(packed, "orient", 0, 0, tiled=True)
    x = edges(spread[:, 0], 2).reshape(devices * local, -1)
    cot = edges(spread[:, 1], 1).reshape(devices * local, -1)
    free = edges((1 - turbine_mask).astype(F32), 1)
    free = windows(jnp.pad(free, ((0, 0), (2, 2))), devices)
    free = lax.dynamic_index_in_dim(free, lax.axis_index("orient"), 0, keepdims=False)
    opened = jnp.broadcast_to(free.reshape(1, -1), (8, (height + 2) * LANES))
    wake, t1, t2 = local_kernel(extent // devices, bases, turn, opened, x, cot)
    wake = lax.all_to_all(wake.reshape(devices, local, -1), "orient", 0, 0, tiled=True)
    wake = wake.reshape(devices, local, height, LANES)[..., 2 : 2 + extent // devices]
    wake = wake.transpose(1, 2, 0, 3).reshape(groups, channels, height, extent)
    t1, t2 = lax.psum((t1, t2), ("orient", "strip"))
    return (wake, unfold(t1, sector) * scale, unfold(t2, neutral) * scale)


def solution(mesh):
    return jax.shard_map(
        shards,
        mesh=mesh,
        in_specs=(
            P("orient", None, "strip", None),
            P(),
            P(),
            P("strip", None),
            P(),
            P("orient", None, "strip", None),
        ),
        out_specs=(P("orient", None, "strip", None), P(), P()),
        check_vma=False,
    )
```

```python
import functools
import math

import jax
import jax.numpy as jnp
from jax import lax
from jax.experimental import pallas as pl
from jax.experimental.pallas import tpu as pltpu
from jax.sharding import PartitionSpec as P

G = 32
HALF = 16
LANES = 128
BF16 = jnp.bfloat16
F32 = jnp.float32


def split_element(sector):
    return sector % HALF, sector // HALF


def selection(rot, ref, mirrored):
    p = lax.broadcasted_iota(jnp.int32, (256, 256), 0)
    q = lax.broadcasted_iota(jnp.int32, (256, 256), 1)
    h = q >> 3
    turned = (rot + (1 - 2 * ref) * (h & 15)) & 15
    side = (ref + (h >> 4)) & 1
    if mirrored:
        turned = (-turned) & 15
        side = 1 - side
    wanted = ((side * HALF + turned) << 3) + (q & 7)
    return jnp.where(p == wanted, 1.0, 0.0).astype(BF16)


def bank_rows(bank, out):
    c = lax.broadcasted_iota(jnp.int32, (8, 256), 0)
    q = lax.broadcasted_iota(jnp.int32, (8, 256), 1)
    spread = jnp.where(c == (q & 7), 1.0, 0.0).astype(BF16)
    lane = lax.broadcasted_iota(jnp.int32, (72, 256), 1) >> 3
    total = jnp.zeros((72, 256), F32)
    for e in range(G):
        wide = dot(bank[e * 72 : (e + 1) * 72, :], spread)
        total = jnp.where(lane == e, wide, total)
    out[...] = total.astype(BF16)


def build_weights(rows, picks, dst, base_ref, flip):
    for s in range(2):
        base_ref[...] = dot(rows[...], picks[s])
        for k in range(9):
            for m in range(2):
                at = k * 256 + m * LANES
                base = base_ref[8 * k : 8 * k + 8, m * LANES : (m + 1) * LANES]
                turned = [base if r == 0 else pltpu.roll(base, 8 * r, 1) for r in range(HALF)]
                if flip is not None:
                    turned = [jnp.where(flip, turned[-r % HALF], turned[r]) for r in range(HALF)]
                for r in range(0, HALF, 2):
                    both = jnp.concatenate([turned[r], turned[r + 1]], axis=0).astype(BF16)
                    row = (s * HALF + r) * 8
                    dst[row : row + 16, at : at + LANES] = both


def fold(product, folded, tap_row, flip):
    for sg in range(2):
        for b in range(3):
            for m in range(2):
                lane = slice(b * 256 + m * LANES, b * 256 + (m + 1) * LANES)
                total = None
                for r in range(HALF):
                    row = (sg * HALF + r) * 8
                    piece = product[row : row + 8, lane]
                    if r > 0:
                        back = pltpu.roll(piece, LANES - 8 * r, 1)
                        if flip is not None:
                            back = jnp.where(flip, pltpu.roll(piece, 8 * r, 1), back)
                        piece = back
                    total = piece if total is None else total + piece
                at = (tap_row * 3 + b) * 8
                folded[sg, at : at + 8, m * LANES : (m + 1) * LANES] = total


def unselect(folded, picks):
    total = None
    for s in range(2):
        rest = folded[s]
        for _ in range(3):
            part = rest.astype(BF16)
            rest = rest - part.astype(F32)
            term = dot_nt(part, picks[s])
            total = term if total is None else total + term
    return total


def shifted(value, by):
    if by == 0:
        return value
    return pltpu.roll(value.astype(F32), by % LANES, 1).astype(BF16)


def stack_shifts(src, dst, first, count, sign):
    for i in range(first, first + count):
        cols = slice(i * LANES, (i + 1) * LANES)
        value = src[:, cols]
        for b in range(3):
            dst[b * 256 : (b + 1) * 256, cols] = shifted(value, sign * (1 - b))


def dot(a, b):
    return jnp.dot(a, b, preferred_element_type=F32)


def dot_nt(a, b):
    return lax.dot_general(a, b, (((1,), (1,)), ((), ())), preferred_element_type=F32)


def compute(width, sector, bank1, bank2, opened, x, cot, wake, shares, w1, w2, w2t, xs, hs, cs, dfac, hid, own, prod, rows, base, pick, folded):
    rot, ref = split_element(sector[0])
    flip = (lax.broadcasted_iota(jnp.int32, (8, LANES), 0) * 0 + ref) == 1
    for s in range(2):
        pick[s] = selection(rot, ref, s == 1)
        pick[2 + s] = selection(0, 0, s == 1)
    bank_rows(bank1, rows)
    build_weights(rows, [pick[0], pick[1]], w1, base, flip)
    bank_rows(bank2, rows)
    build_weights(rows, [pick[2], pick[3]], w2, base, None)
    for k in range(9):
        cols = slice(k * 256, (k + 1) * 256)
        w2t[:, cols] = dot_nt(pick[2], w2[:, cols]).astype(BF16)
    lane = lax.broadcasted_iota(jnp.int32, (256, LANES), 1)
    inner = (lane >= 2) & (lane < 2 + width)
    stack_shifts(x, xs, 0, 12, 1)
    for n in range(5):
        total = sum(
            dot(w1[:, a * 768 : (a + 1) * 768], xs[:, (2 * n + a) * LANES : (2 * n + a + 2) * LANES])
            for a in range(3)
        )
        cols = slice(2 * n * LANES, (2 * n + 2) * LANES)
        free = opened[0:1, cols]
        sig = jax.nn.sigmoid(total)
        hid[:, cols] = (total * sig * free).astype(BF16)
        dfac[:, cols] = free * sig * (1.0 + total * (1.0 - sig))
    stack_shifts(hid, hs, 0, 10, 1)
    for n in range(4):
        total = sum(
            dot(w2[:, a * 768 : (a + 1) * 768], hs[:, (2 * n + a) * LANES : (2 * n + a + 2) * LANES])
            for a in range(3)
        )
        wake[:, 2 * n * LANES : (2 * n + 2) * LANES] = total.astype(BF16)
    stack_shifts(cot, cs, 0, 10, -1)
    for i in range(8):
        value = cot[:, (i + 1) * LANES : (i + 2) * LANES].astype(F32)
        own[:, i * LANES : (i + 1) * LANES] = jnp.where(inner, value, 0.0).astype(BF16)
    for a in range(3):
        prod[...] = dot_nt(own[...], hs[:, a * LANES : (a + 8) * LANES])
        fold(prod, folded, a, None)
    shares[72:144, :] = unselect(folded, [pick[2], pick[3]])
    for n in range(4):
        total = sum(
            dot(
                w2t[:, a * 768 : (a + 1) * 768],
                cs[:, (2 * n + 2 - a) * LANES : (2 * n + 4 - a) * LANES],
            )
            for a in range(3)
        )
        cols = slice((2 * n + 1) * LANES, (2 * n + 3) * LANES)
        total = total * dfac[:, cols]
        for i in range(2):
            value = jnp.where(inner, total[:, i * LANES : (i + 1) * LANES], 0.0)
            own[:, (2 * n + i) * LANES : (2 * n + i + 1) * LANES] = value.astype(BF16)
    for a in range(3):
        prod[...] = dot_nt(own[...], xs[:, (a + 1) * LANES : (a + 9) * LANES])
        fold(prod, folded, a, flip)
    shares[0:72, :] = unselect(folded, [pick[0], pick[1]])


def expand(scale, shares, one, two):
    for layer, out in enumerate((one, two)):
        value = shares[layer * 72 : (layer + 1) * 72, :] * scale
        for e in range(G):
            out[e * 72 : (e + 1) * 72, :] = value[:, e * 8 : e * 8 + 8]


def expand_kernel(scale, shares):
    vmem = pl.BlockSpec(memory_space=pltpu.VMEM)
    out = jax.ShapeDtypeStruct((G * 72, 8), F32)
    return pl.pallas_call(
        functools.partial(expand, scale),
        out_shape=(out, out),
        in_specs=[vmem],
        out_specs=(vmem, vmem),
        compiler_params=pltpu.CompilerParams(vmem_limit_bytes=32 * 1024 * 1024),
    )(shares)


def pack(width, x, cot, out, wide):
    local, height, extent = x.shape
    phases = LANES // width
    for which, src in enumerate((x, cot)):
        wide[...] = src[...].astype(F32)
        for r in range(height):
            row = jnp.concatenate([wide[:, r, :], jnp.zeros((local, LANES), F32)], axis=1)
            for phase in range(phases):
                moved = pltpu.roll(row, (2 - width * phase) % (extent + LANES), 1).astype(BF16)
                for m in range(extent // LANES):
                    piece = moved[:, m * LANES : (m + 1) * LANES]
                    out[m * phases + phase, which, :, r * LANES : (r + 1) * LANES] = piece


def pack_kernel(width, x, cot):
    local, height, extent = x.shape
    vmem = pl.BlockSpec(memory_space=pltpu.VMEM)
    return pl.pallas_call(
        functools.partial(pack, width),
        out_shape=jax.ShapeDtypeStruct((extent // width, 2, local, height * LANES), BF16),
        in_specs=[vmem] * 2,
        out_specs=vmem,
        scratch_shapes=[pltpu.VMEM((local, height, extent), F32)],
        compiler_params=pltpu.CompilerParams(vmem_limit_bytes=32 * 1024 * 1024),
    )(x, cot)


def local_kernel(width, sector, bank1, bank2, opened, x, cot):
    vmem = pl.BlockSpec(memory_space=pltpu.VMEM)
    smem = pl.BlockSpec(memory_space=pltpu.SMEM)
    return pl.pallas_call(
        functools.partial(compute, width),
        out_shape=(
            jax.ShapeDtypeStruct((256, 8 * LANES), BF16),
            jax.ShapeDtypeStruct((144, 256), F32),
        ),
        in_specs=[smem] + [vmem] * 5,
        out_specs=(vmem,) * 2,
        scratch_shapes=[
            pltpu.VMEM((256, 2304), BF16),
            pltpu.VMEM((256, 2304), BF16),
            pltpu.VMEM((256, 2304), BF16),
            pltpu.VMEM((768, 12 * LANES), BF16),
            pltpu.VMEM((768, 10 * LANES), BF16),
            pltpu.VMEM((768, 10 * LANES), BF16),
            pltpu.VMEM((256, 10 * LANES), F32),
            pltpu.VMEM((256, 10 * LANES), BF16),
            pltpu.VMEM((256, 8 * LANES), BF16),
            pltpu.VMEM((256, 768), F32),
            pltpu.VMEM((72, 256), BF16),
            pltpu.VMEM((72, 256), F32),
            pltpu.VMEM((4, 256, 256), BF16),
            pltpu.VMEM((2, 72, 256), F32),
        ],
        compiler_params=pltpu.CompilerParams(vmem_limit_bytes=48 * 1024 * 1024),
    )(sector, bank1, bank2, opened, x, cot)


def edges(rows, width):
    count = lax.axis_size("strip")
    height = rows.shape[-2]
    up = [(i, i + 1) for i in range(count - 1)]
    down = [(i + 1, i) for i in range(count - 1)]
    before = lax.ppermute(rows[..., height - width :, :], "strip", up)
    after = lax.ppermute(rows[..., :width, :], "strip", down)
    return jnp.concatenate([before, rows, after], axis=-2)


def summed(shares):
    axes = ("orient", "strip")
    count = lax.axis_size("orient") * lax.axis_size("strip")
    parts = lax.all_to_all(shares.reshape(count, -1), axes, 0, 0, tiled=True)
    part = jnp.broadcast_to(jnp.sum(parts, axis=0, keepdims=True), parts.shape)
    return lax.all_to_all(part, axes, 0, 0, tiled=True).reshape(shares.shape)


def shards(inflow_field, kernel_one, kernel_two, turbine_mask, wind_sector, wake_cotangent):
    groups, channels, height, extent = inflow_field.shape
    local = groups * channels
    devices = lax.axis_size("orient")
    width = extent // devices
    scale = 1.0 / math.sqrt(G * height * lax.axis_size("strip") * extent)
    shape = (local, height, extent)
    packed = pack_kernel(width, inflow_field.reshape(shape), wake_cotangent.reshape(shape))
    free = jnp.pad((1 - turbine_mask).astype(F32), ((0, 0), (2, LANES)))
    free = lax.dynamic_slice_in_dim(free, lax.axis_index("orient") * width, LANES, axis=1)
    free = jnp.where(jnp.arange(LANES) < width + 4, free, 0.0)
    free = edges(free, 1)
    opened = jnp.broadcast_to(free.reshape(1, -1), (8, (height + 2) * LANES))
    spread = lax.all_to_all(packed, "orient", 0, 0, tiled=True)
    spread = spread.reshape(devices, 2, local, height, LANES)
    x = edges(spread[:, 0], 2).reshape(devices * local, -1)
    cot = edges(spread[:, 1], 1).reshape(devices * local, -1)
    bank1, bank2 = kernel_one.reshape(-1, channels), kernel_two.reshape(-1, channels)
    wake, shares = local_kernel(width, wind_sector, bank1, bank2, opened, x, cot)
    wake = lax.all_to_all(wake.reshape(devices, local, -1), "orient", 0, 0, tiled=True)
    wake = wake.reshape(devices, local, height, LANES)[..., 2 : 2 + extent // devices]
    wake = wake.transpose(1, 2, 0, 3).reshape(groups, channels, height, extent)
    one, two = expand_kernel(scale, summed(shares))
    return (wake, one.reshape(kernel_one.shape), two.reshape(kernel_two.shape))


def solution(mesh):
    return jax.shard_map(
        shards,
        mesh=mesh,
        in_specs=(
            P("orient", None, "strip", None),
            P(),
            P(),
            P("strip", None),
            P(),
            P("orient", None, "strip", None),
        ),
        out_specs=(P("orient", None, "strip", None), P(), P()),
        check_vma=False,
    )
```

```python
import functools
import math

import jax
import jax.numpy as jnp
from jax import lax
from jax.experimental import pallas as pl
from jax.experimental.pallas import tpu as pltpu
from jax.sharding import PartitionSpec as P

G = 32
HALF = 16
LANES = 128
BF16 = jnp.bfloat16
F32 = jnp.float32


def split_element(sector):
    return sector % HALF, sector // HALF


def selection(rot, ref, mirrored):
    p = lax.broadcasted_iota(jnp.int32, (256, 256), 0)
    q = lax.broadcasted_iota(jnp.int32, (256, 256), 1)
    h = q >> 3
    turned = (rot + (1 - 2 * ref) * (h & 15)) & 15
    side = (ref + (h >> 4)) & 1
    if mirrored:
        turned = (-turned) & 15
        side = 1 - side
    wanted = ((side * HALF + turned) << 3) + (q & 7)
    return jnp.where(p == wanted, 1.0, 0.0).astype(BF16)


def bank_rows(bank, out):
    c = lax.broadcasted_iota(jnp.int32, (8, 256), 0)
    q = lax.broadcasted_iota(jnp.int32, (8, 256), 1)
    spread = jnp.where(c == (q & 7), 1.0, 0.0).astype(BF16)
    lane = lax.broadcasted_iota(jnp.int32, (72, 256), 1) >> 3
    total = jnp.zeros((72, 256), F32)
    for e in range(G):
        wide = dot(bank[e * 72 : (e + 1) * 72, :], spread)
        total = jnp.where(lane == e, wide, total)
    out[...] = total.astype(BF16)


def build_weights(rows, picks, dst, base_ref, flip):
    for s in range(2):
        base_ref[...] = dot(rows[...], picks[s])
        for k in range(9):
            for m in range(2):
                at = k * 256 + m * LANES
                base = base_ref[8 * k : 8 * k + 8, m * LANES : (m + 1) * LANES]
                turned = [base if r == 0 else pltpu.roll(base, 8 * r, 1) for r in range(HALF)]
                if flip is not None:
                    turned = [jnp.where(flip, turned[-r % HALF], turned[r]) for r in range(HALF)]
                for r in range(0, HALF, 2):
                    both = jnp.concatenate([turned[r], turned[r + 1]], axis=0).astype(BF16)
                    row = (s * HALF + r) * 8
                    dst[row : row + 16, at : at + LANES] = both


def fold(product, folded, tap_row, flip):
    for sg in range(2):
        for b in range(3):
            for m in range(2):
                lane = slice(b * 256 + m * LANES, b * 256 + (m + 1) * LANES)
                total = None
                for r in range(HALF):
                    row = (sg * HALF + r) * 8
                    piece = product[row : row + 8, lane]
                    if r > 0:
                        back = pltpu.roll(piece, LANES - 8 * r, 1)
                        if flip is not None:
                            back = jnp.where(flip, pltpu.roll(piece, 8 * r, 1), back)
                        piece = back
                    total = piece if total is None else total + piece
                at = (tap_row * 3 + b) * 8
                folded[sg, at : at + 8, m * LANES : (m + 1) * LANES] = total


def unselect(folded, picks):
    total = None
    for s in range(2):
        rest = folded[s]
        for _ in range(3):
            part = rest.astype(BF16)
            rest = rest - part.astype(F32)
            term = dot_nt(part, picks[s])
            total = term if total is None else total + term
    return total


def shifted(value, by):
    if by == 0:
        return value
    return pltpu.roll(value.astype(F32), by % LANES, 1).astype(BF16)


def stack_shifts(src, dst, first, count, sign):
    for i in range(first, first + count):
        cols = slice(i * LANES, (i + 1) * LANES)
        value = src[:, cols]
        for b in range(3):
            dst[b * 256 : (b + 1) * 256, cols] = shifted(value, sign * (1 - b))


def dot(a, b):
    return jnp.dot(a, b, preferred_element_type=F32)


def dot_nt(a, b):
    return lax.dot_general(a, b, (((1,), (1,)), ((), ())), preferred_element_type=F32)


def compute(width, sector, bank1, bank2, opened, x, cot, wake, shares, w1, w2, w2t, xs, hs, cs, dfac, hid, own, prod, rows, base, pick, folded):
    rot, ref = split_element(sector[0])
    flip = (lax.broadcasted_iota(jnp.int32, (8, LANES), 0) * 0 + ref) == 1
    for s in range(2):
        pick[s] = selection(rot, ref, s == 1)
        pick[2 + s] = selection(0, 0, s == 1)
    bank_rows(bank1, rows)
    build_weights(rows, [pick[0], pick[1]], w1, base, flip)
    bank_rows(bank2, rows)
    build_weights(rows, [pick[2], pick[3]], w2, base, None)
    for k in range(9):
        cols = slice(k * 256, (k + 1) * 256)
        w2t[:, cols] = dot_nt(pick[2], w2[:, cols]).astype(BF16)
    lane = lax.broadcasted_iota(jnp.int32, (256, LANES), 1)
    inner = (lane >= 2) & (lane < 2 + width)
    stack_shifts(x, xs, 0, 12, 1)
    for n in range(5):
        total = sum(
            dot(w1[:, a * 768 : (a + 1) * 768], xs[:, (2 * n + a) * LANES : (2 * n + a + 2) * LANES])
            for a in range(3)
        )
        cols = slice(2 * n * LANES, (2 * n + 2) * LANES)
        free = opened[0:1, cols]
        sig = jax.nn.sigmoid(total)
        hid[:, cols] = (total * sig * free).astype(BF16)
        dfac[:, cols] = free * sig * (1.0 + total * (1.0 - sig))
    stack_shifts(hid, hs, 0, 10, 1)
    for n in range(4):
        total = sum(
            dot(w2[:, a * 768 : (a + 1) * 768], hs[:, (2 * n + a) * LANES : (2 * n + a + 2) * LANES])
            for a in range(3)
        )
        wake[:, 2 * n * LANES : (2 * n + 2) * LANES] = total.astype(BF16)
    stack_shifts(cot, cs, 0, 10, -1)
    for i in range(8):
        value = cot[:, (i + 1) * LANES : (i + 2) * LANES].astype(F32)
        own[:, i * LANES : (i + 1) * LANES] = jnp.where(inner, value, 0.0).astype(BF16)
    for a in range(3):
        prod[...] = dot_nt(own[...], hs[:, a * LANES : (a + 8) * LANES])
        fold(prod, folded, a, None)
    shares[72:144, :] = unselect(folded, [pick[2], pick[3]])
    for n in range(4):
        total = sum(
            dot(
                w2t[:, a * 768 : (a + 1) * 768],
                cs[:, (2 * n + 2 - a) * LANES : (2 * n + 4 - a) * LANES],
            )
            for a in range(3)
        )
        cols = slice((2 * n + 1) * LANES, (2 * n + 3) * LANES)
        total = total * dfac[:, cols]
        for i in range(2):
            value = jnp.where(inner, total[:, i * LANES : (i + 1) * LANES], 0.0)
            own[:, (2 * n + i) * LANES : (2 * n + i + 1) * LANES] = value.astype(BF16)
    for a in range(3):
        prod[...] = dot_nt(own[...], xs[:, (a + 1) * LANES : (a + 9) * LANES])
        fold(prod, folded, a, flip)
    shares[0:72, :] = unselect(folded, [pick[0], pick[1]])


def expand(scale, shares, one, two):
    for layer, out in enumerate((one, two)):
        value = shares[layer * 72 : (layer + 1) * 72, :] * scale
        for e in range(G):
            out[e * 72 : (e + 1) * 72, :] = value[:, e * 8 : e * 8 + 8]


def expand_kernel(scale, shares):
    vmem = pl.BlockSpec(memory_space=pltpu.VMEM)
    out = jax.ShapeDtypeStruct((G * 72, 8), F32)
    return pl.pallas_call(
        functools.partial(expand, scale),
        out_shape=(out, out),
        in_specs=[vmem],
        out_specs=(vmem, vmem),
        compiler_params=pltpu.CompilerParams(vmem_limit_bytes=32 * 1024 * 1024),
    )(shares)


def pack(width, x, cot, out, wide):
    local, height, extent = x.shape
    phases = LANES // width
    for which, src in enumerate((x, cot)):
        wide[...] = src[...].astype(F32)
        for r in range(height):
            row = jnp.concatenate([wide[:, r, :], jnp.zeros((local, LANES), F32)], axis=1)
            for phase in range(phases):
                moved = pltpu.roll(row, (2 - width * phase) % (extent + LANES), 1).astype(BF16)
                for m in range(extent // LANES):
                    piece = moved[:, m * LANES : (m + 1) * LANES]
                    out[m * phases + phase, which, :, r * LANES : (r + 1) * LANES] = piece


def pack_kernel(width, x, cot):
    local, height, extent = x.shape
    vmem = pl.BlockSpec(memory_space=pltpu.VMEM)
    return pl.pallas_call(
        functools.partial(pack, width),
        out_shape=jax.ShapeDtypeStruct((extent // width, 2, local, height * LANES), BF16),
        in_specs=[vmem] * 2,
        out_specs=vmem,
        scratch_shapes=[pltpu.VMEM((local, height, extent), F32)],
        compiler_params=pltpu.CompilerParams(vmem_limit_bytes=32 * 1024 * 1024),
    )(x, cot)


def local_kernel(width, sector, bank1, bank2, opened, x, cot):
    vmem = pl.BlockSpec(memory_space=pltpu.VMEM)
    smem = pl.BlockSpec(memory_space=pltpu.SMEM)
    return pl.pallas_call(
        functools.partial(compute, width),
        out_shape=(
            jax.ShapeDtypeStruct((256, 8 * LANES), BF16),
            jax.ShapeDtypeStruct((144, 256), F32),
        ),
        in_specs=[smem] + [vmem] * 5,
        out_specs=(vmem,) * 2,
        scratch_shapes=[
            pltpu.VMEM((256, 2304), BF16),
            pltpu.VMEM((256, 2304), BF16),
            pltpu.VMEM((256, 2304), BF16),
            pltpu.VMEM((768, 12 * LANES), BF16),
            pltpu.VMEM((768, 10 * LANES), BF16),
            pltpu.VMEM((768, 10 * LANES), BF16),
            pltpu.VMEM((256, 10 * LANES), F32),
            pltpu.VMEM((256, 10 * LANES), BF16),
            pltpu.VMEM((256, 8 * LANES), BF16),
            pltpu.VMEM((256, 768), F32),
            pltpu.VMEM((72, 256), BF16),
            pltpu.VMEM((72, 256), F32),
            pltpu.VMEM((4, 256, 256), BF16),
            pltpu.VMEM((2, 72, 256), F32),
        ],
        compiler_params=pltpu.CompilerParams(vmem_limit_bytes=48 * 1024 * 1024),
    )(sector, bank1, bank2, opened, x, cot)


def remote(src, dst, send, recv, **to):
    return pltpu.make_async_remote_copy(
        src_ref=src,
        dst_ref=dst,
        send_sem=send,
        recv_sem=recv,
        device_id=to,
        device_id_type=pl.DeviceIdType.MESH,
    )


def greet(**to):
    barrier = pltpu.get_barrier_semaphore()
    pl.semaphore_signal(barrier, inc=1, device_id=to, device_id_type=pl.DeviceIdType.MESH)


def exchange_in(count, strips, packed, free, x, cot, opened, send, recv, edge_send, edge_recv):
    me, z = lax.axis_index("orient"), lax.axis_index("strip")
    for j in range(1, count):
        greet(orient=lax.rem(me + j, count))
    greet(strip=lax.rem(z + strips - 1, strips))
    greet(strip=lax.rem(z + 1, strips))
    pl.semaphore_wait(pltpu.get_barrier_semaphore(), count + 1)
    height = free.shape[1] // LANES
    inner = ((x, 2), (cot, 1))
    copies = []
    for which, (out, rim) in enumerate(inner):
        for j in range(1, count):
            peer = lax.rem(me + j, count)
            copy = remote(
                packed.at[peer, which],
                out.at[me, :, rim * LANES : (rim + height) * LANES],
                send.at[which, j],
                recv.at[which, j],
                orient=peer,
            )
            copy.start()
            copies.append(copy)

    def rims(kind, out, rim, lead):
        size = rim * LANES
        end = (rim + height) * LANES
        up = remote(
            out.at[lead + (slice(size, 2 * size),)],
            out.at[lead + (slice(end, end + size),)],
            edge_send.at[0, kind],
            edge_recv.at[0, kind],
            strip=lax.rem(z + strips - 1, strips),
        )
        down = remote(
            out.at[lead + (slice(end - size, end),)],
            out.at[lead + (slice(0, size),)],
            edge_send.at[1, kind],
            edge_recv.at[1, kind],
            strip=lax.rem(z + 1, strips),
        )

        @pl.when(z > 0)
        def _():
            up.start()

        @pl.when(z == 0)
        def _():
            out[lead + (slice(0, size),)] = jnp.zeros(out.shape[:-1] + (size,), out.dtype)

        @pl.when(z < strips - 1)
        def _():
            down.start()

        @pl.when(z == strips - 1)
        def _():
            out[lead + (slice(end, end + size),)] = jnp.zeros(out.shape[:-1] + (size,), out.dtype)

        return up, down

    opened[:, LANES : (1 + height) * LANES] = free[...]
    pairs = [rims(2, opened, 1, (slice(None),))]
    for which, (out, rim) in enumerate(inner):
        out[me, :, rim * LANES : (rim + height) * LANES] = packed[me, which]
    for which, (out, rim) in enumerate(inner):
        for copy in copies[which * (count - 1) : (which + 1) * (count - 1)]:
            copy.wait_recv()
        pairs.append(rims(which, out, rim, (slice(None), slice(None))))
    for copy in copies:
        copy.wait_send()
    for up, down in pairs:

        @pl.when(z > 0)
        def _():
            up.wait_send()
            down.wait_recv()

        @pl.when(z < strips - 1)
        def _():
            down.wait_send()
            up.wait_recv()


def exchange_in_kernel(packed, free):
    vmem = pl.BlockSpec(memory_space=pltpu.VMEM)
    count, _, local, lanes = packed.shape
    return pl.pallas_call(
        functools.partial(exchange_in, count, lax.axis_size("strip")),
        out_shape=(
            jax.ShapeDtypeStruct((count, local, lanes + 4 * LANES), BF16),
            jax.ShapeDtypeStruct((count, local, lanes + 2 * LANES), BF16),
            jax.ShapeDtypeStruct((8, lanes + 2 * LANES), F32),
        ),
        in_specs=[vmem] * 2,
        out_specs=(vmem,) * 3,
        scratch_shapes=[
            pltpu.SemaphoreType.DMA((2, count)),
            pltpu.SemaphoreType.DMA((2, count)),
            pltpu.SemaphoreType.DMA((2, 3)),
            pltpu.SemaphoreType.DMA((2, 3)),
        ],
        compiler_params=pltpu.CompilerParams(
            collective_id=0, has_side_effects=True, vmem_limit_bytes=32 * 1024 * 1024
        ),
    )(packed, free)


def exchange_out(count, strips, wake, shares, out, full, parts, totals, done, send, recv, z_send, z_recv):
    me, z = lax.axis_index("orient"), lax.axis_index("strip")
    for j in range(1, count):
        greet(orient=lax.rem(me + j, count))
    for j in range(1, strips):
        greet(strip=lax.rem(z + j, strips))
    pl.semaphore_wait(pltpu.get_barrier_semaphore(), count + strips - 2)

    def to_all(kind, src_of, dst):
        copies = []
        for j in range(1, count):
            peer = lax.rem(me + j, count)
            copy = remote(
                src_of(peer), dst.at[me], send.at[kind, j], recv.at[kind, j], orient=peer
            )
            copy.start()
            copies.append(copy)
        return copies

    first = to_all(0, lambda peer: shares.at[peer], parts)
    waking = to_all(1, lambda peer: wake.at[peer], out)
    parts[me] = shares[me]
    out[me] = wake[me]
    for copy in first:
        copy.wait_recv()
    total = parts[0]
    for i in range(1, count):
        total = total + parts[i]
    totals[z] = total
    second = []
    for j in range(1, strips):
        copy = remote(
            totals.at[z], totals.at[z], z_send.at[j], z_recv.at[j], strip=lax.rem(z + j, strips)
        )
        copy.start()
        second.append(copy)
    for copy in second:
        copy.wait_recv()
    total = totals[0]
    for i in range(1, strips):
        total = total + totals[i]
    done[...] = total
    full[me] = total
    third = to_all(2, lambda peer: done, full)
    for copy in third + waking:
        copy.wait_recv()
    for copy in first + waking + second + third:
        copy.wait_send()


def exchange_out_kernel(wake, shares):
    vmem = pl.BlockSpec(memory_space=pltpu.VMEM)
    count, strips = wake.shape[0], lax.axis_size("strip")
    part = shares.shape[1:]
    return pl.pallas_call(
        functools.partial(exchange_out, count, strips),
        out_shape=(
            jax.ShapeDtypeStruct(wake.shape, wake.dtype),
            jax.ShapeDtypeStruct(shares.shape, F32),
        ),
        in_specs=[vmem] * 2,
        out_specs=(vmem,) * 2,
        scratch_shapes=[
            pltpu.VMEM((count,) + part, F32),
            pltpu.VMEM((strips,) + part, F32),
            pltpu.VMEM(part, F32),
            pltpu.SemaphoreType.DMA((3, count)),
            pltpu.SemaphoreType.DMA((3, count)),
            pltpu.SemaphoreType.DMA((strips,)),
            pltpu.SemaphoreType.DMA((strips,)),
        ],
        compiler_params=pltpu.CompilerParams(
            collective_id=1, has_side_effects=True, vmem_limit_bytes=32 * 1024 * 1024
        ),
    )(wake, shares)


def shards(inflow_field, kernel_one, kernel_two, turbine_mask, wind_sector, wake_cotangent):
    groups, channels, height, extent = inflow_field.shape
    local = groups * channels
    devices = lax.axis_size("orient")
    width = extent // devices
    scale = 1.0 / math.sqrt(G * height * lax.axis_size("strip") * extent)
    shape = (local, height, extent)
    packed = pack_kernel(width, inflow_field.reshape(shape), wake_cotangent.reshape(shape))
    free = jnp.pad((1 - turbine_mask).astype(F32), ((0, 0), (2, LANES)))
    free = lax.dynamic_slice_in_dim(free, lax.axis_index("orient") * width, LANES, axis=1)
    free = jnp.where(jnp.arange(LANES) < width + 4, free, 0.0)
    free = jnp.broadcast_to(free.reshape(1, -1), (8, height * LANES))
    x, cot, opened = exchange_in_kernel(packed, free)
    x = x.reshape(devices * local, -1)
    cot = cot.reshape(devices * local, -1)
    bank1, bank2 = kernel_one.reshape(-1, channels), kernel_two.reshape(-1, channels)
    wake, shares = local_kernel(width, wind_sector, bank1, bank2, opened, x, cot)
    wake, shares = exchange_out_kernel(
        wake.reshape(devices, local, -1), shares.reshape(devices, -1, LANES)
    )
    wake = wake.reshape(devices, local, height, LANES)[..., 2 : 2 + extent // devices]
    wake = wake.transpose(1, 2, 0, 3).reshape(groups, channels, height, extent)
    one, two = expand_kernel(scale, shares.reshape(144, 256))
    return (wake, one.reshape(kernel_one.shape), two.reshape(kernel_two.shape))


def solution(mesh):
    return jax.shard_map(
        shards,
        mesh=mesh,
        in_specs=(
            P("orient", None, "strip", None),
            P(),
            P(),
            P("strip", None),
            P(),
            P("orient", None, "strip", None),
        ),
        out_specs=(P("orient", None, "strip", None), P(), P()),
        check_vma=False,
    )
```

```python
import functools
import math

import jax
import jax.numpy as jnp
from jax import lax
from jax.experimental import pallas as pl
from jax.experimental.pallas import tpu as pltpu
from jax.sharding import PartitionSpec as P

G = 32
HALF = 16
LANES = 128
BF16 = jnp.bfloat16
F32 = jnp.float32


def split_element(sector):
    return sector % HALF, sector // HALF


def selection(rot, ref, mirrored):
    p = lax.broadcasted_iota(jnp.int32, (256, 256), 0)
    q = lax.broadcasted_iota(jnp.int32, (256, 256), 1)
    h = q >> 3
    turned = (rot + (1 - 2 * ref) * (h & 15)) & 15
    side = (ref + (h >> 4)) & 1
    if mirrored:
        turned = (-turned) & 15
        side = 1 - side
    wanted = ((side * HALF + turned) << 3) + (q & 7)
    return jnp.where(p == wanted, 1.0, 0.0).astype(BF16)


def bank_rows(bank, out):
    c = lax.broadcasted_iota(jnp.int32, (8, 256), 0)
    q = lax.broadcasted_iota(jnp.int32, (8, 256), 1)
    spread = jnp.where(c == (q & 7), 1.0, 0.0).astype(BF16)
    lane = lax.broadcasted_iota(jnp.int32, (72, 256), 1) >> 3
    total = jnp.zeros((72, 256), F32)
    for e in range(G):
        wide = dot(bank[e * 72 : (e + 1) * 72, :], spread)
        total = jnp.where(lane == e, wide, total)
    out[...] = total.astype(BF16)


def build_weights(rows, picks, dst, base_ref, flip):
    for s in range(2):
        base_ref[...] = dot(rows[...], picks[s])
        for k in range(9):
            for m in range(2):
                at = k * 256 + m * LANES
                base = base_ref[8 * k : 8 * k + 8, m * LANES : (m + 1) * LANES]
                turned = [base if r == 0 else pltpu.roll(base, 8 * r, 1) for r in range(HALF)]
                if flip is not None:
                    turned = [jnp.where(flip, turned[-r % HALF], turned[r]) for r in range(HALF)]
                for r in range(0, HALF, 2):
                    both = jnp.concatenate([turned[r], turned[r + 1]], axis=0).astype(BF16)
                    row = (s * HALF + r) * 8
                    dst[row : row + 16, at : at + LANES] = both


def fold(product, folded, tap_row, flip):
    for sg in range(2):
        for b in range(3):
            for m in range(2):
                lane = slice(b * 256 + m * LANES, b * 256 + (m + 1) * LANES)
                total = None
                for r in range(HALF):
                    row = (sg * HALF + r) * 8
                    piece = product[row : row + 8, lane]
                    if r > 0:
                        back = pltpu.roll(piece, LANES - 8 * r, 1)
                        if flip is not None:
                            back = jnp.where(flip, pltpu.roll(piece, 8 * r, 1), back)
                        piece = back
                    total = piece if total is None else total + piece
                at = (tap_row * 3 + b) * 8
                folded[sg, at : at + 8, m * LANES : (m + 1) * LANES] = total


def unselect(folded, picks):
    total = None
    for s in range(2):
        rest = folded[s]
        for _ in range(3):
            part = rest.astype(BF16)
            rest = rest - part.astype(F32)
            term = dot_nt(part, picks[s])
            total = term if total is None else total + term
    return total


def shifted(value, by):
    if by == 0:
        return value
    return pltpu.roll(value.astype(F32), by % LANES, 1).astype(BF16)


def stack_shifts(src, dst, first, count, sign):
    for i in range(first, first + count):
        cols = slice(i * LANES, (i + 1) * LANES)
        value = src[:, cols]
        for b in range(3):
            dst[b * 256 : (b + 1) * 256, cols] = shifted(value, sign * (1 - b))


def dot(a, b):
    return jnp.dot(a, b, preferred_element_type=F32)


def dot_nt(a, b):
    return lax.dot_general(a, b, (((1,), (1,)), ((), ())), preferred_element_type=F32)


def compute(width, sector, bank1, bank2, opened, x, cot, wake, shares, w1, w2, w2t, xs, hs, cs, dfac, hid, own, prod, rows, base, pick, folded):
    rot, ref = split_element(sector[0])
    flip = (lax.broadcasted_iota(jnp.int32, (8, LANES), 0) * 0 + ref) == 1
    for s in range(2):
        pick[s] = selection(rot, ref, s == 1)
        pick[2 + s] = selection(0, 0, s == 1)
    bank_rows(bank1, rows)
    build_weights(rows, [pick[0], pick[1]], w1, base, flip)
    bank_rows(bank2, rows)
    build_weights(rows, [pick[2], pick[3]], w2, base, None)
    for k in range(9):
        cols = slice(k * 256, (k + 1) * 256)
        w2t[:, cols] = dot_nt(pick[2], w2[:, cols]).astype(BF16)
    lane = lax.broadcasted_iota(jnp.int32, (256, LANES), 1)
    inner = (lane >= 2) & (lane < 2 + width)
    stack_shifts(x, xs, 0, 12, 1)
    for n in range(5):
        total = sum(
            dot(w1[:, a * 768 : (a + 1) * 768], xs[:, (2 * n + a) * LANES : (2 * n + a + 2) * LANES])
            for a in range(3)
        )
        cols = slice(2 * n * LANES, (2 * n + 2) * LANES)
        free = opened[0:1, cols]
        sig = jax.nn.sigmoid(total)
        hid[:, cols] = (total * sig * free).astype(BF16)
        dfac[:, cols] = free * sig * (1.0 + total * (1.0 - sig))
    stack_shifts(hid, hs, 0, 10, 1)
    for n in range(4):
        total = sum(
            dot(w2[:, a * 768 : (a + 1) * 768], hs[:, (2 * n + a) * LANES : (2 * n + a + 2) * LANES])
            for a in range(3)
        )
        wake[:, 2 * n * LANES : (2 * n + 2) * LANES] = total.astype(BF16)
    stack_shifts(cot, cs, 0, 10, -1)
    for i in range(8):
        value = cot[:, (i + 1) * LANES : (i + 2) * LANES].astype(F32)
        own[:, i * LANES : (i + 1) * LANES] = jnp.where(inner, value, 0.0).astype(BF16)
    for a in range(3):
        prod[...] = dot_nt(own[...], hs[:, a * LANES : (a + 8) * LANES])
        fold(prod, folded, a, None)
    shares[72:144, :] = unselect(folded, [pick[2], pick[3]])
    for n in range(4):
        total = sum(
            dot(
                w2t[:, a * 768 : (a + 1) * 768],
                cs[:, (2 * n + 2 - a) * LANES : (2 * n + 4 - a) * LANES],
            )
            for a in range(3)
        )
        cols = slice((2 * n + 1) * LANES, (2 * n + 3) * LANES)
        total = total * dfac[:, cols]
        for i in range(2):
            value = jnp.where(inner, total[:, i * LANES : (i + 1) * LANES], 0.0)
            own[:, (2 * n + i) * LANES : (2 * n + i + 1) * LANES] = value.astype(BF16)
    for a in range(3):
        prod[...] = dot_nt(own[...], xs[:, (a + 1) * LANES : (a + 9) * LANES])
        fold(prod, folded, a, flip)
    shares[0:72, :] = unselect(folded, [pick[0], pick[1]])


def expand(scale, shares, one, two):
    for layer, out in enumerate((one, two)):
        value = shares[layer * 72 : (layer + 1) * 72, :] * scale
        for e in range(G):
            out[e] = value[:, e * 8 : e * 8 + 8].reshape(9, 8, 8)


def expand_kernel(scale, shares):
    vmem = pl.BlockSpec(memory_space=pltpu.VMEM)
    out = jax.ShapeDtypeStruct((G, 9, 8, 8), F32)
    return pl.pallas_call(
        functools.partial(expand, scale),
        out_shape=(out, out),
        in_specs=[vmem],
        out_specs=(vmem, vmem),
        compiler_params=pltpu.CompilerParams(vmem_limit_bytes=32 * 1024 * 1024),
    )(shares)


def pack(width, x, cot, out, wide):
    local, height, extent = x.shape
    phases = LANES // width
    for which, src in enumerate((x, cot)):
        wide[...] = src[...].astype(F32)
        for r in range(height):
            row = jnp.concatenate([wide[:, r, :], jnp.zeros((local, LANES), F32)], axis=1)
            for phase in range(phases):
                moved = pltpu.roll(row, (2 - width * phase) % (extent + LANES), 1).astype(BF16)
                for m in range(extent // LANES):
                    piece = moved[:, m * LANES : (m + 1) * LANES]
                    out[m * phases + phase, which, :, r * LANES : (r + 1) * LANES] = piece


def pack_kernel(width, x, cot):
    local, height, extent = x.shape
    vmem = pl.BlockSpec(memory_space=pltpu.VMEM)
    return pl.pallas_call(
        functools.partial(pack, width),
        out_shape=jax.ShapeDtypeStruct((extent // width, 2, local, height * LANES), BF16),
        in_specs=[vmem] * 2,
        out_specs=vmem,
        scratch_shapes=[pltpu.VMEM((local, height, extent), F32)],
        compiler_params=pltpu.CompilerParams(vmem_limit_bytes=32 * 1024 * 1024),
    )(x, cot)


def local_kernel(width, sector, bank1, bank2, opened, x, cot):
    vmem = pl.BlockSpec(memory_space=pltpu.VMEM)
    smem = pl.BlockSpec(memory_space=pltpu.SMEM)
    return pl.pallas_call(
        functools.partial(compute, width),
        out_shape=(
            jax.ShapeDtypeStruct((256, 8 * LANES), BF16),
            jax.ShapeDtypeStruct((144, 256), F32),
        ),
        in_specs=[smem] + [vmem] * 5,
        out_specs=(vmem,) * 2,
        scratch_shapes=[
            pltpu.VMEM((256, 2304), BF16),
            pltpu.VMEM((256, 2304), BF16),
            pltpu.VMEM((256, 2304), BF16),
            pltpu.VMEM((768, 12 * LANES), BF16),
            pltpu.VMEM((768, 10 * LANES), BF16),
            pltpu.VMEM((768, 10 * LANES), BF16),
            pltpu.VMEM((256, 10 * LANES), F32),
            pltpu.VMEM((256, 10 * LANES), BF16),
            pltpu.VMEM((256, 8 * LANES), BF16),
            pltpu.VMEM((256, 768), F32),
            pltpu.VMEM((72, 256), BF16),
            pltpu.VMEM((72, 256), F32),
            pltpu.VMEM((4, 256, 256), BF16),
            pltpu.VMEM((2, 72, 256), F32),
        ],
        compiler_params=pltpu.CompilerParams(vmem_limit_bytes=48 * 1024 * 1024),
    )(sector, bank1, bank2, opened, x, cot)


def remote(src, dst, send, recv, **to):
    return pltpu.make_async_remote_copy(
        src_ref=src,
        dst_ref=dst,
        send_sem=send,
        recv_sem=recv,
        device_id=to,
        device_id_type=pl.DeviceIdType.MESH,
    )


def greet(**to):
    barrier = pltpu.get_barrier_semaphore()
    pl.semaphore_signal(barrier, inc=1, device_id=to, device_id_type=pl.DeviceIdType.MESH)


def exchange_in(count, strips, packed, free, x, cot, opened, send, recv, edge_send, edge_recv):
    me, z = lax.axis_index("orient"), lax.axis_index("strip")
    for j in range(1, count):
        greet(orient=lax.rem(me + j, count))
    greet(strip=lax.rem(z + strips - 1, strips))
    greet(strip=lax.rem(z + 1, strips))
    pl.semaphore_wait(pltpu.get_barrier_semaphore(), count + 1)
    height = free.shape[1] // LANES
    inner = ((x, 2), (cot, 1))
    copies = []
    for which, (out, rim) in enumerate(inner):
        for j in range(1, count):
            peer = lax.rem(me + j, count)
            copy = remote(
                packed.at[peer, which],
                out.at[me, :, rim * LANES : (rim + height) * LANES],
                send.at[which, j],
                recv.at[which, j],
                orient=peer,
            )
            copy.start()
            copies.append(copy)

    def rims(kind, out, rim, lead):
        size = rim * LANES
        end = (rim + height) * LANES
        up = remote(
            out.at[lead + (slice(size, 2 * size),)],
            out.at[lead + (slice(end, end + size),)],
            edge_send.at[0, kind],
            edge_recv.at[0, kind],
            strip=lax.rem(z + strips - 1, strips),
        )
        down = remote(
            out.at[lead + (slice(end - size, end),)],
            out.at[lead + (slice(0, size),)],
            edge_send.at[1, kind],
            edge_recv.at[1, kind],
            strip=lax.rem(z + 1, strips),
        )

        @pl.when(z > 0)
        def _():
            up.start()

        @pl.when(z == 0)
        def _():
            out[lead + (slice(0, size),)] = jnp.zeros(out.shape[:-1] + (size,), out.dtype)

        @pl.when(z < strips - 1)
        def _():
            down.start()

        @pl.when(z == strips - 1)
        def _():
            out[lead + (slice(end, end + size),)] = jnp.zeros(out.shape[:-1] + (size,), out.dtype)

        return up, down

    opened[:, LANES : (1 + height) * LANES] = free[...]
    pairs = [rims(2, opened, 1, (slice(None),))]
    for which, (out, rim) in enumerate(inner):
        out[me, :, rim * LANES : (rim + height) * LANES] = packed[me, which]
    for which, (out, rim) in enumerate(inner):
        for copy in copies[which * (count - 1) : (which + 1) * (count - 1)]:
            copy.wait_recv()
        pairs.append(rims(which, out, rim, (slice(None), slice(None))))
    for copy in copies:
        copy.wait_send()
    for up, down in pairs:

        @pl.when(z > 0)
        def _():
            up.wait_send()
            down.wait_recv()

        @pl.when(z < strips - 1)
        def _():
            down.wait_send()
            up.wait_recv()


def exchange_in_kernel(packed, free):
    vmem = pl.BlockSpec(memory_space=pltpu.VMEM)
    count, _, local, lanes = packed.shape
    return pl.pallas_call(
        functools.partial(exchange_in, count, lax.axis_size("strip")),
        out_shape=(
            jax.ShapeDtypeStruct((count, local, lanes + 4 * LANES), BF16),
            jax.ShapeDtypeStruct((count, local, lanes + 2 * LANES), BF16),
            jax.ShapeDtypeStruct((8, lanes + 2 * LANES), F32),
        ),
        in_specs=[vmem] * 2,
        out_specs=(vmem,) * 3,
        scratch_shapes=[
            pltpu.SemaphoreType.DMA((2, count)),
            pltpu.SemaphoreType.DMA((2, count)),
            pltpu.SemaphoreType.DMA((2, 3)),
            pltpu.SemaphoreType.DMA((2, 3)),
        ],
        compiler_params=pltpu.CompilerParams(
            collective_id=0, has_side_effects=True, vmem_limit_bytes=32 * 1024 * 1024
        ),
    )(packed, free)


def exchange_out(count, strips, wake, shares, out, full, parts, totals, done, send, recv, z_send, z_recv):
    me, z = lax.axis_index("orient"), lax.axis_index("strip")
    for j in range(1, count):
        greet(orient=lax.rem(me + j, count))
    for j in range(1, strips):
        greet(strip=lax.rem(z + j, strips))
    pl.semaphore_wait(pltpu.get_barrier_semaphore(), count + strips - 2)

    def to_all(kind, src_of, dst):
        copies = []
        for j in range(1, count):
            peer = lax.rem(me + j, count)
            copy = remote(
                src_of(peer), dst.at[me], send.at[kind, j], recv.at[kind, j], orient=peer
            )
            copy.start()
            copies.append(copy)
        return copies

    first = to_all(0, lambda peer: shares.at[peer], parts)
    waking = to_all(1, lambda peer: wake.at[peer], out)
    parts[me] = shares[me]
    out[me] = wake[me]
    for copy in first:
        copy.wait_recv()
    total = parts[0]
    for i in range(1, count):
        total = total + parts[i]
    totals[z] = total
    second = []
    for j in range(1, strips):
        copy = remote(
            totals.at[z], totals.at[z], z_send.at[j], z_recv.at[j], strip=lax.rem(z + j, strips)
        )
        copy.start()
        second.append(copy)
    for copy in second:
        copy.wait_recv()
    total = totals[0]
    for i in range(1, strips):
        total = total + totals[i]
    done[...] = total
    full[me] = total
    third = to_all(2, lambda peer: done, full)
    for copy in third + waking:
        copy.wait_recv()
    for copy in first + waking + second + third:
        copy.wait_send()


def exchange_out_kernel(wake, shares):
    vmem = pl.BlockSpec(memory_space=pltpu.VMEM)
    count, strips = wake.shape[0], lax.axis_size("strip")
    part = shares.shape[1:]
    return pl.pallas_call(
        functools.partial(exchange_out, count, strips),
        out_shape=(
            jax.ShapeDtypeStruct(wake.shape, wake.dtype),
            jax.ShapeDtypeStruct(shares.shape, F32),
        ),
        in_specs=[vmem] * 2,
        out_specs=(vmem,) * 2,
        scratch_shapes=[
            pltpu.VMEM((count,) + part, F32),
            pltpu.VMEM((strips,) + part, F32),
            pltpu.VMEM(part, F32),
            pltpu.SemaphoreType.DMA((3, count)),
            pltpu.SemaphoreType.DMA((3, count)),
            pltpu.SemaphoreType.DMA((strips,)),
            pltpu.SemaphoreType.DMA((strips,)),
        ],
        compiler_params=pltpu.CompilerParams(
            collective_id=1, has_side_effects=True, vmem_limit_bytes=32 * 1024 * 1024
        ),
    )(wake, shares)


def shards(inflow_field, kernel_one, kernel_two, turbine_mask, wind_sector, wake_cotangent):
    groups, channels, height, extent = inflow_field.shape
    local = groups * channels
    devices = lax.axis_size("orient")
    width = extent // devices
    scale = 1.0 / math.sqrt(G * height * lax.axis_size("strip") * extent)
    shape = (local, height, extent)
    packed = pack_kernel(width, inflow_field.reshape(shape), wake_cotangent.reshape(shape))
    free = jnp.pad((1 - turbine_mask).astype(F32), ((0, 0), (2, LANES)))
    free = lax.dynamic_slice_in_dim(free, lax.axis_index("orient") * width, LANES, axis=1)
    free = jnp.where(jnp.arange(LANES) < width + 4, free, 0.0)
    free = jnp.broadcast_to(free.reshape(1, -1), (8, height * LANES))
    x, cot, opened = exchange_in_kernel(packed, free)
    x = x.reshape(devices * local, -1)
    cot = cot.reshape(devices * local, -1)
    bank1, bank2 = kernel_one.reshape(-1, channels), kernel_two.reshape(-1, channels)
    wake, shares = local_kernel(width, wind_sector, bank1, bank2, opened, x, cot)
    wake, shares = exchange_out_kernel(
        wake.reshape(devices, local, -1), shares.reshape(devices, -1, LANES)
    )
    wake = wake.reshape(devices, local, height, LANES)[..., 2 : 2 + extent // devices]
    wake = wake.transpose(1, 2, 0, 3).reshape(groups, channels, height, extent)
    one, two = expand_kernel(scale, shares.reshape(144, 256))
    return (wake, one, two)


def solution(mesh):
    return jax.shard_map(
        shards,
        mesh=mesh,
        in_specs=(
            P("orient", None, "strip", None),
            P(),
            P(),
            P("strip", None),
            P(),
            P("orient", None, "strip", None),
        ),
        out_specs=(P("orient", None, "strip", None), P(), P()),
        check_vma=False,
    )
```
